512 devices in a mesh: row: 32 (over z, y_lo, core), col: 16 (over x, y_hi).
Axes of the slice: x: 4, y: 8 (y_hi: 4, y_lo: 2; y = y_hi * 2 + y_lo), z: 8, core: 2. Of those that a mesh axis runs over, the one named last changes fastest.
Arguments:
- trailing: float32 [2, 8192, 4, 4096], P(None, 'row', None, 'col'), may hold values from -6 to 6
- panel: float32 [2, 8192, 256], P(None, 'row', 'col'), may hold values from -1 to 1
- factor_inverse: float32 [256, 256], replicated, may hold values from -2 to 3, as said below
Outputs:
- updated: float32 [2, 8192, 4, 4096], P(None, 'row', None, 'col')
- factor_panel: float32 [2, 8192, 256], P(None, 'row', 'col')
The draws below stay inside these ranges and needn't reach their ends.
Inputs may be any that keep to these rules, and one draw needn't show every extreme that they name: `factor_inverse`: lower triangular; diagonal entries between 1 and 3.
All inputs are finite; a program needn't handle non-finite values.
Results may differ from the reference program's by a relative error of at most 0.00007.
Values sent between devices are 32-bit elements; how exact they have to be, the bound alone decides.
No kernel may reach another device: no remote copies, remote signals or barrier semaphores. Data moves between devices by JAX's collectives and lax.ppermute only.
A program may use at most 64 MiB of HBM per device.

```python
import math
import jax
import jax.numpy as jnp
from jax import lax

B = 256
RT = 2
CT = 4
N_ROW = 32
N_COL = 16


def draw_factor_inverse(key, part):
    key = jax.random.fold_in(key, 11)
    first, second = jax.random.split(key, 2)
    rows = jnp.arange(B)[:, None]
    cols = jnp.arange(B)[None, :]
    off = jnp.clip(jax.random.normal(first, (B, B), jnp.float32), -6.0, 6.0) / math.sqrt(B)
    diagonal = jnp.exp(jax.random.uniform(second, (B,), jnp.float32, 0.0, math.log(3.0)))
    return jnp.where(rows > cols, off, 0.0) + jnp.diag(diagonal)


def block_scale(key, dims, pieces, low, high):
    loudness, own = 1.0, jax.random.fold_in(key, 6)
    for axis_at, blocks in pieces:
        steps = jnp.exp(jax.random.uniform(jax.random.fold_in(own, axis_at), (blocks,), jnp.float32, low / len(pieces), high / len(pieces)))
        loudness = loudness * jnp.repeat(steps, dims[axis_at] // blocks).reshape([-1 if axis == axis_at else 1 for axis in range(len(dims))])
    return loudness


def gaussian(own_key, extent, width, most, shards=(), dtype=jnp.bfloat16):
    array = width * jax.random.normal(own_key, extent, jnp.float32)
    if shards:
        array = array * block_scale(own_key, extent, shards, -0.22, 0.18)
    return jnp.clip(array, -most, most).astype(dtype)


def setup_inputs(seed: int = 0) -> dict:
    splits = jax.random.split(jax.random.key(seed), 4)
    trailing = gaussian(splits[0], (RT, N_ROW * B, CT, N_COL * B), 1.0, 6.0, ((1, 32), (3, 16)), jnp.float32)
    panel = gaussian(splits[1], (RT, N_ROW * B, B), 0.0625, 1.0, ((1, 32), (2, 16)), jnp.float32)
    factor_inverse = draw_factor_inverse(jax.random.fold_in(splits[3], 71), 0)
    return dict(trailing=trailing, panel=panel, factor_inverse=factor_inverse)


def reference(trailing, panel, factor_inverse):
    order = RT * N_ROW * B
    whole = trailing.reshape(order, order)
    column = panel.reshape(order, B)
    factor = jnp.dot(column, factor_inverse.T, preferred_element_type=jnp.float32, precision=lax.Precision.HIGHEST)
    product = jnp.dot(factor, factor.T, preferred_element_type=jnp.float32, precision=lax.Precision.HIGHEST)
    updated = (whole - product).reshape(RT, N_ROW * B, CT, N_COL * B)
    return updated, factor.reshape(RT, N_ROW * B, B)
```

```python
import functools

import jax
import jax.numpy as jnp
from jax import lax
from jax.experimental import pallas as pl
from jax.experimental.pallas import tpu as pltpu
from jax.sharding import Mesh
from jax.sharding import PartitionSpec as P

AXES = ("zg", "z0", "yl", "core", "x", "yh")
SIZES = (4, 2, 2, 2, 4, 4)
ROW, COL = AXES[:4], AXES[4:]


def place(zg, z0, yl, core, x, yh):
    at = 0
    for size, i in zip(SIZES, (zg, z0, yl, core, x, yh)):
        at = at * size + i
    return at


def to_columns():
    pairs = []
    for zg in range(4):
        for z0 in range(2):
            for yl in range(2):
                for core in range(2):
                    for x in range(4):
                        for yh in range(4):
                            z = 2 * zg + z0
                            to = (yh + z + 2 * core + yl + x) % 4
                            target = place(to, x // 2, x % 2, z // 4, z % 4, 2 * yl + core)
                            pairs.append((place(zg, z0, yl, core, x, yh), target))
    return pairs


def gather(block, axes, n):
    many = jnp.broadcast_to(block[None], (n,) + block.shape)
    return lax.all_to_all(many, axes, 0, 0, tiled=True)


def split(value):
    high = value.astype(jnp.bfloat16)
    low = (value - high.astype(jnp.float32)).astype(jnp.bfloat16)
    return high, low


def product(left, right):
    dot = functools.partial(jnp.dot, preferred_element_type=jnp.float32)
    return dot(left[0], right[0]) + (dot(left[0], right[1]) + dot(left[1], right[0]))


def own_kernel(at_ref, rows_ref, inverse_ref, high_ref, low_ref, panel_ref):
    inverse = split(inverse_ref[...])
    start = pl.multiple_of(at_ref[0] * 16, 16)
    for t in range(2):
        factor = product(inverse, split(rows_ref[:, t].reshape(256, 256)))
        high_ref[t], low_ref[t] = split(factor.T)
        panel_ref[t] = product(
            split(inverse_ref[pl.ds(start, 16), :]), split(rows_ref[:, t].reshape(256, 256))
        )


def update_kernel(at_ref, trailing_ref, high_ref, low_ref, mine_ref, other_ref, inverse_ref, out_ref, right_high, right_low):
    @pl.when((pl.program_id(0) == 0) & (pl.program_id(1) == 0))
    def _():
        inverse = split(inverse_ref[...])
        for ref, half in ((mine_ref, at_ref[1]), (other_ref, 1 - at_ref[1])):
            for t in range(2):
                factor = product(inverse, split(ref[:, t].reshape(256, 256)))
                high, low = split(factor)
                for part in range(2):
                    start = pl.multiple_of((part * 4 + t * 2 + half) * 128, 128)
                    right_high[:, pl.ds(start, 128)] = high[:, part * 128 : part * 128 + 128]
                    right_low[:, pl.ds(start, 128)] = low[:, part * 128 : part * 128 + 128]

    total = product((high_ref[0], low_ref[0]), (right_high[...], right_low[...]))
    rows = total.shape[0]
    out_ref[0] = trailing_ref[0] - total.reshape(rows, 8, 128)


def on_device(trailing, panel, factor_inverse):
    col = lax.axis_index(COL)
    core = lax.axis_index("core")
    at = jnp.stack([col, core]).astype(jnp.int32)
    sliver = jnp.swapaxes(panel, 1, 2)
    quarter = gather(sliver, ("yh",), 4)
    (quarter,) = lax.optimization_barrier((quarter,))
    sent = lax.ppermute(quarter, AXES, to_columns())
    own = gather(quarter, ("x",), 4)
    sent, own = lax.optimization_barrier((sent, own))
    mine = gather(sent, ("z0", "yl"), 4)
    own, mine = own.reshape(16, 2, 16, 256), mine.reshape(16, 2, 16, 256)
    other = lax.ppermute(mine, "core", [(0, 1), (1, 0)])

    smem = pl.BlockSpec(memory_space=pltpu.SMEM)
    vmem = pl.BlockSpec(memory_space=pltpu.VMEM)
    high, low, factor_panel = pl.pallas_call(
        own_kernel,
        out_shape=[
            jax.ShapeDtypeStruct((2, 256, 256), jnp.bfloat16),
            jax.ShapeDtypeStruct((2, 256, 256), jnp.bfloat16),
            jax.ShapeDtypeStruct((2, 16, 256), jnp.float32),
        ],
        in_specs=[smem, vmem, vmem],
        out_specs=[vmem, vmem, vmem],
        compiler_params=pltpu.CompilerParams(vmem_limit_bytes=32 * 1024 * 1024),
    )(at, own, factor_inverse)

    whole = trailing.reshape(2, 256, 4, 2, 128).swapaxes(2, 3).reshape(2, 256, 8, 128)
    rows = 128
    updated = pl.pallas_call(
        update_kernel,
        grid=(2, 256 // rows),
        out_shape=jax.ShapeDtypeStruct((2, 256, 8, 128), jnp.float32),
        in_specs=[
            smem,
            pl.BlockSpec((1, rows, 8, 128), lambda t, i: (t, i, 0, 0)),
            pl.BlockSpec((1, rows, 256), lambda t, i: (t, i, 0)),
            pl.BlockSpec((1, rows, 256), lambda t, i: (t, i, 0)),
            vmem,
            vmem,
            vmem,
        ],
        out_specs=pl.BlockSpec((1, rows, 8, 128), lambda t, i: (t, i, 0, 0)),
        scratch_shapes=[
            pltpu.VMEM((256, 1024), jnp.bfloat16),
            pltpu.VMEM((256, 1024), jnp.bfloat16),
        ],
        compiler_params=pltpu.CompilerParams(vmem_limit_bytes=32 * 1024 * 1024),
    )(at, whole, high, low, mine, other, factor_inverse)
    updated = updated.reshape(2, 256, 2, 4, 128).swapaxes(2, 3).reshape(2, 256, 4, 256)
    return updated, jnp.swapaxes(factor_panel, 1, 2)


def solution(mesh):
    fine = Mesh(mesh.devices.reshape(SIZES), AXES)
    specs = (P(None, ROW, None, COL), P(None, ROW, COL), P())
    return jax.shard_map(
        on_device, mesh=fine, in_specs=specs, out_specs=specs[:2], check_vma=False
    )
```

```python
import functools

import jax
import jax.numpy as jnp
from jax import lax
from jax.experimental import pallas as pl
from jax.experimental.pallas import tpu as pltpu
from jax.sharding import Mesh
from jax.sharding import PartitionSpec as P

AXES = ("z", "yl", "core", "x", "yh")
SIZES = (8, 2, 2, 4, 4)
ROW, COL = AXES[:3], AXES[3:]
ROWS = 128


def to_columns():
    pairs = []
    for p in range(32):
        for q in range(16):
            pairs.append((p * 16 + q, (q * 2 + p // 16) * 16 + p % 16))
    return pairs


def split(value):
    high = value.astype(jnp.bfloat16)
    low = (value - high.astype(jnp.float32)).astype(jnp.bfloat16)
    return high, low


def product(left, right):
    dot = functools.partial(jnp.dot, preferred_element_type=jnp.float32)
    return dot(left[0], right[0]) + (dot(left[0], right[1]) + dot(left[1], right[0]))


def own_kernel(at_ref, rows_ref, inverse_ref, high_ref, low_ref, panel_ref):
    inverse = split(inverse_ref[...])
    start = pl.multiple_of(at_ref[0] * 16, 16)
    for t in range(2):
        factor = product(inverse, split(rows_ref[:, t].reshape(256, 256)))
        high_ref[t], low_ref[t] = split(factor.T)
        panel_ref[t] = product(
            split(inverse_ref[pl.ds(start, 16), :]), split(rows_ref[:, t].reshape(256, 256))
        )


def update_kernel(at_ref, trailing_ref, high_ref, low_ref, mine_ref, other_ref, inverse_ref, out_ref, right_high, right_low, done, sems):
    inverse = split(inverse_ref[...])
    for ref, half in ((mine_ref, at_ref[1]), (other_ref, 1 - at_ref[1])):
        for t in range(2):
            high, low = split(product(inverse, split(ref[:, t].reshape(256, 256))))
            for part in range(2):
                start = pl.multiple_of((part * 4 + t * 2 + half) * 128, 128)
                right_high[:, pl.ds(start, 128)] = high[:, part * 128 : part * 128 + 128]
                right_low[:, pl.ds(start, 128)] = low[:, part * 128 : part * 128 + 128]
    right = (right_high[...], right_low[...])
    copies = []
    for t in range(2):
        for i in range(256 // ROWS):
            rows = pl.ds(i * ROWS, ROWS)
            total = product((high_ref[t, rows], low_ref[t, rows]), right)
            done[t, rows] = trailing_ref[t, rows] - total.reshape(ROWS, 8, 128)
            copy = pltpu.make_async_copy(done.at[t, rows], out_ref.at[t, rows], sems.at[len(copies)])
            copy.start()
            copies.append(copy)
    for copy in copies:
        copy.wait()


def on_device(trailing, panel, factor_inverse):
    col = lax.axis_index(COL)
    core = lax.axis_index("core")
    at = jnp.stack([col, core]).astype(jnp.int32)
    sliver = jnp.swapaxes(panel, 1, 2)
    sent = lax.ppermute(sliver, AXES, to_columns())
    quarter = lax.all_gather(sliver, "yh")
    sent, quarter = lax.optimization_barrier((sent, quarter))
    many = jnp.broadcast_to(sent[None], (16, 2, 16, 256))
    mine = lax.all_to_all(many, ("z", "yl"), 0, 0, tiled=True)
    own = lax.all_gather(quarter, "x").reshape(16, 2, 16, 256)
    mine, own = lax.optimization_barrier((mine, own))
    other = lax.ppermute(mine, "core", [(0, 1), (1, 0)])

    smem = pl.BlockSpec(memory_space=pltpu.SMEM)
    vmem = pl.BlockSpec(memory_space=pltpu.VMEM)
    high, low, factor_panel = pl.pallas_call(
        own_kernel,
        out_shape=[
            jax.ShapeDtypeStruct((2, 256, 256), jnp.bfloat16),
            jax.ShapeDtypeStruct((2, 256, 256), jnp.bfloat16),
            jax.ShapeDtypeStruct((2, 16, 256), jnp.float32),
        ],
        in_specs=[smem, vmem, vmem],
        out_specs=[vmem, vmem, vmem],
        compiler_params=pltpu.CompilerParams(vmem_limit_bytes=32 * 1024 * 1024),
    )(at, own, factor_inverse)

    whole = trailing.reshape(2, 256, 4, 2, 128).swapaxes(2, 3).reshape(2, 256, 8, 128)
    updated = pl.pallas_call(
        update_kernel,
        out_shape=jax.ShapeDtypeStruct((2, 256, 8, 128), jnp.float32),
        in_specs=[smem] + [vmem] * 6,
        out_specs=pl.BlockSpec(memory_space=pl.ANY),
        scratch_shapes=[
            pltpu.VMEM((256, 1024), jnp.bfloat16),
            pltpu.VMEM((256, 1024), jnp.bfloat16),
            pltpu.VMEM((2, 256, 8, 128), jnp.float32),
            pltpu.SemaphoreType.DMA((512 // ROWS,)),
        ],
        compiler_params=pltpu.CompilerParams(vmem_limit_bytes=32 * 1024 * 1024),
    )(at, whole, high, low, mine, other, factor_inverse)
    updated = updated.reshape(2, 256, 2, 4, 128).swapaxes(2, 3).reshape(2, 256, 4, 256)
    return updated, jnp.swapaxes(factor_panel, 1, 2)


def solution(mesh):
    fine = Mesh(mesh.devices.reshape(SIZES), AXES)
    specs = (P(None, ROW, None, COL), P(None, ROW, COL), P())
    return jax.shard_map(
        on_device, mesh=fine, in_specs=specs, out_specs=specs[:2], check_vma=False
    )
```

```python
import functools

import jax
import jax.numpy as jnp
from jax import lax
from jax.experimental import pallas as pl
from jax.experimental.pallas import tpu as pltpu
from jax.sharding import Mesh
from jax.sharding import PartitionSpec as P

AXES = ("z", "yl", "core", "x", "yh")
SIZES = (8, 2, 2, 4, 4)
ROW, COL = AXES[:3], AXES[3:]
ROWS = 128


def to_columns():
    pairs = []
    for p in range(32):
        for q in range(16):
            pairs.append((p * 16 + q, (q * 2 + p // 16) * 16 + p % 16))
    return pairs


def gather_pairs(block, axis):
    block = lax.all_gather(block, axis, axis=0, tiled=True, axis_index_groups=[[0, 1], [2, 3]])
    return lax.all_gather(block, axis, axis=0, tiled=True, axis_index_groups=[[0, 3], [1, 2]])


def split(value):
    high = value.astype(jnp.bfloat16)
    low = (value - high.astype(jnp.float32)).astype(jnp.bfloat16)
    return high, low


def product(left, right):
    dot = functools.partial(jnp.dot, preferred_element_type=jnp.float32)
    return dot(left[0], right[0]) + (dot(left[0], right[1]) + dot(left[1], right[0]))


def own_kernel(at_ref, rows_ref, inverse_ref, high_ref, low_ref, panel_ref):
    inverse = split(inverse_ref[...])
    start = pl.multiple_of(at_ref[0] * 16, 16)
    for t in range(2):
        factor = product(inverse, split(rows_ref[:, t].reshape(256, 256)))
        high_ref[t], low_ref[t] = split(factor.T)
        panel_ref[t] = product(
            split(inverse_ref[pl.ds(start, 16), :]), split(rows_ref[:, t].reshape(256, 256))
        )


def update_kernel(at_ref, trailing_ref, high_ref, low_ref, mine_ref, other_ref, inverse_ref, out_ref, right_high, right_low, done, sems):
    inverse = split(inverse_ref[...])
    for ref, half in ((mine_ref, at_ref[1]), (other_ref, 1 - at_ref[1])):
        for t in range(2):
            high, low = split(product(inverse, split(ref[:, t].reshape(256, 256))))
            for part in range(2):
                start = pl.multiple_of((part * 4 + t * 2 + half) * 128, 128)
                right_high[:, pl.ds(start, 128)] = high[:, part * 128 : part * 128 + 128]
                right_low[:, pl.ds(start, 128)] = low[:, part * 128 : part * 128 + 128]
    right = (right_high[...], right_low[...])
    copies = []
    for t in range(2):
        for i in range(256 // ROWS):
            rows = pl.ds(i * ROWS, ROWS)
            total = product((high_ref[t, rows], low_ref[t, rows]), right)
            done[t, rows] = trailing_ref[t, rows] - total.reshape(ROWS, 8, 128)
            copy = pltpu.make_async_copy(done.at[t, rows], out_ref.at[t, rows], sems.at[len(copies)])
            copy.start()
            copies.append(copy)
    for copy in copies:
        copy.wait()


def on_device(trailing, panel, factor_inverse):
    col = lax.axis_index(COL)
    core = lax.axis_index("core")
    at = jnp.stack([col, core]).astype(jnp.int32)
    sliver = jnp.swapaxes(panel, 1, 2)
    sent = lax.ppermute(sliver, AXES, to_columns())
    quarter = gather_pairs(sliver[None], "yh")
    sent, quarter = lax.optimization_barrier((sent, quarter))
    many = jnp.broadcast_to(sent[None], (16, 2, 16, 256))
    mine = lax.all_to_all(many, ("z", "yl"), 0, 0, tiled=True)
    own = lax.all_gather(quarter, "x", axis=0, tiled=True)
    mine, own = lax.optimization_barrier((mine, own))
    other = lax.ppermute(mine, "core", [(0, 1), (1, 0)])

    smem = pl.BlockSpec(memory_space=pltpu.SMEM)
    vmem = pl.BlockSpec(memory_space=pltpu.VMEM)
    high, low, factor_panel = pl.pallas_call(
        own_kernel,
        out_shape=[
            jax.ShapeDtypeStruct((2, 256, 256), jnp.bfloat16),
            jax.ShapeDtypeStruct((2, 256, 256), jnp.bfloat16),
            jax.ShapeDtypeStruct((2, 16, 256), jnp.float32),
        ],
        in_specs=[smem, vmem, vmem],
        out_specs=[vmem, vmem, vmem],
        compiler_params=pltpu.CompilerParams(vmem_limit_bytes=32 * 1024 * 1024),
    )(at, own, factor_inverse)

    whole = trailing.reshape(2, 256, 4, 2, 128).swapaxes(2, 3).reshape(2, 256, 8, 128)
    updated = pl.pallas_call(
        update_kernel,
        out_shape=jax.ShapeDtypeStruct((2, 256, 8, 128), jnp.float32),
        in_specs=[smem] + [vmem] * 6,
        out_specs=pl.BlockSpec(memory_space=pl.ANY),
        scratch_shapes=[
            pltpu.VMEM((256, 1024), jnp.bfloat16),
            pltpu.VMEM((256, 1024), jnp.bfloat16),
            pltpu.VMEM((2, 256, 8, 128), jnp.float32),
            pltpu.SemaphoreType.DMA((512 // ROWS,)),
        ],
        compiler_params=pltpu.CompilerParams(vmem_limit_bytes=32 * 1024 * 1024),
    )(at, whole, high, low, mine, other, factor_inverse)
    updated = updated.reshape(2, 256, 2, 4, 128).swapaxes(2, 3).reshape(2, 256, 4, 256)
    return updated, jnp.swapaxes(factor_panel, 1, 2)


def solution(mesh):
    fine = Mesh(mesh.devices.reshape(SIZES), AXES)
    specs = (P(None, ROW, None, COL), P(None, ROW, COL), P())
    return jax.shard_map(
        on_device, mesh=fine, in_specs=specs, out_specs=specs[:2], check_vma=False
    )
```

```python
import functools

import jax
import jax.numpy as jnp
from jax import lax
from jax.experimental import pallas as pl
from jax.experimental.pallas import tpu as pltpu
from jax.sharding import Mesh
from jax.sharding import PartitionSpec as P

AXES = ("z", "yl", "core", "x", "yh")
SIZES = (8, 2, 2, 4, 4)
ROW, COL = AXES[:3], AXES[3:]
ROWS = 128


def to_columns():
    pairs = []
    for p in range(32):
        for q in range(16):
            pairs.append((p * 16 + q, (q * 2 + p // 16) * 16 + p % 16))
    return pairs


def gather_pairs(block, axis):
    block = lax.all_gather(block, axis, axis=0, tiled=True, axis_index_groups=[[0, 1], [2, 3]])
    return lax.all_gather(block, axis, axis=0, tiled=True, axis_index_groups=[[0, 3], [1, 2]])


def split(value):
    high = value.astype(jnp.bfloat16)
    low = (value - high.astype(jnp.float32)).astype(jnp.bfloat16)
    return high, low


def product(left, right):
    dot = functools.partial(jnp.dot, preferred_element_type=jnp.float32)
    return dot(left[0], right[0]) + (dot(left[0], right[1]) + dot(left[1], right[0]))


def own_kernel(at_ref, rows_ref, mine_ref, inverse_ref, high_ref, low_ref, right_high_ref, right_low_ref, panel_ref):
    inverse = split(inverse_ref[...])
    start = pl.multiple_of(at_ref[0] * 16, 16)
    for t in range(2):
        rows = split(rows_ref[:, t].reshape(256, 256))
        high_ref[t], low_ref[t] = split(product(inverse, rows).T)
        panel_ref[t] = product(split(inverse_ref[pl.ds(start, 16), :]), rows)
    for t in range(2):
        right_high_ref[t], right_low_ref[t] = split(product(inverse, split(mine_ref[:, t].reshape(256, 256))))


def update_kernel(at_ref, trailing_ref, high_ref, low_ref, mine_high, mine_low, other_ref, inverse_ref, out_ref, right_high, right_low, done, sems):
    def place(t, half, high, low):
        for part in range(2):
            start = pl.multiple_of((part * 4 + t * 2 + half) * 128, 128)
            right_high[:, pl.ds(start, 128)] = high[:, part * 128 : part * 128 + 128]
            right_low[:, pl.ds(start, 128)] = low[:, part * 128 : part * 128 + 128]

    inverse = split(inverse_ref[...])
    for t in range(2):
        place(t, at_ref[1], mine_high[t], mine_low[t])
        place(t, 1 - at_ref[1], *split(product(inverse, split(other_ref[:, t].reshape(256, 256)))))
    right = (right_high[...], right_low[...])
    copies = []
    for t in range(2):
        for i in range(256 // ROWS):
            rows = pl.ds(i * ROWS, ROWS)
            total = product((high_ref[t, rows], low_ref[t, rows]), right)
            for part in range(2):
                rows = pl.ds(i * ROWS + part * 64, 64)
                done[t, rows] = trailing_ref[t, rows] - total[part * 64 : part * 64 + 64].reshape(64, 8, 128)
                copy = pltpu.make_async_copy(done.at[t, rows], out_ref.at[t, rows], sems.at[len(copies)])
                copy.start()
                copies.append(copy)
    for copy in copies:
        copy.wait()


def on_device(trailing, panel, factor_inverse):
    col = lax.axis_index(COL)
    core = lax.axis_index("core")
    at = jnp.stack([col, core]).astype(jnp.int32)
    sliver = jnp.swapaxes(panel, 1, 2)
    sent = lax.ppermute(sliver, AXES, to_columns())
    quarter = gather_pairs(sliver[None], "yh")
    sent, quarter = lax.optimization_barrier((sent, quarter))
    many = jnp.broadcast_to(sent[None], (16, 2, 16, 256))
    mine = lax.all_to_all(many, ("z", "yl"), 0, 0, tiled=True)
    own = lax.all_gather(quarter, "x", axis=0, tiled=True)
    mine, own = lax.optimization_barrier((mine, own))
    other = lax.ppermute(mine, "core", [(0, 1), (1, 0)])

    smem = pl.BlockSpec(memory_space=pltpu.SMEM)
    vmem = pl.BlockSpec(memory_space=pltpu.VMEM)
    square = jax.ShapeDtypeStruct((2, 256, 256), jnp.bfloat16)
    high, low, right_high, right_low, factor_panel = pl.pallas_call(
        own_kernel,
        out_shape=[square] * 4 + [jax.ShapeDtypeStruct((2, 16, 256), jnp.float32)],
        in_specs=[smem, vmem, vmem, vmem],
        out_specs=[vmem] * 5,
        compiler_params=pltpu.CompilerParams(vmem_limit_bytes=32 * 1024 * 1024),
    )(at, own, mine, factor_inverse)

    whole = trailing.reshape(2, 256, 4, 2, 128).swapaxes(2, 3).reshape(2, 256, 8, 128)
    updated = pl.pallas_call(
        update_kernel,
        out_shape=jax.ShapeDtypeStruct((2, 256, 8, 128), jnp.float32),
        in_specs=[smem] + [vmem] * 7,
        out_specs=pl.BlockSpec(memory_space=pl.ANY),
        scratch_shapes=[
            pltpu.VMEM((256, 1024), jnp.bfloat16),
            pltpu.VMEM((256, 1024), jnp.bfloat16),
            pltpu.VMEM((2, 256, 8, 128), jnp.float32),
            pltpu.SemaphoreType.DMA((512 // 64,)),
        ],
        compiler_params=pltpu.CompilerParams(vmem_limit_bytes=32 * 1024 * 1024),
    )(at, whole, high, low, right_high, right_low, other, factor_inverse)
    updated = updated.reshape(2, 256, 2, 4, 128).swapaxes(2, 3).reshape(2, 256, 4, 256)
    return updated, jnp.swapaxes(factor_panel, 1, 2)


def solution(mesh):
    fine = Mesh(mesh.devices.reshape(SIZES), AXES)
    specs = (P(None, ROW, None, COL), P(None, ROW, COL), P())
    return jax.shard_map(
        on_device, mesh=fine, in_specs=specs, out_specs=specs[:2], check_vma=False
    )
```

```python
import functools

import jax
import jax.numpy as jnp
from jax import lax
from jax.experimental import pallas as pl
from jax.experimental.pallas import tpu as pltpu
from jax.sharding import Mesh
from jax.sharding import PartitionSpec as P

AXES = ("z", "yl", "core", "x", "yh")
SIZES = (8, 2, 2, 4, 4)
ROW, COL = AXES[:3], AXES[3:]
ROWS = 128


def to_columns():
    pairs = []
    for p in range(32):
        for q in range(16):
            pairs.append((p * 16 + q, (q * 2 + p // 16) * 16 + p % 16))
    return pairs


def gather_pairs(block, axis):
    block = lax.all_gather(block, axis, axis=0, tiled=True, axis_index_groups=[[0, 1], [2, 3]])
    return lax.all_gather(block, axis, axis=0, tiled=True, axis_index_groups=[[0, 3], [1, 2]])


def split(value):
    high = value.astype(jnp.bfloat16)
    low = (value - high.astype(jnp.float32)).astype(jnp.bfloat16)
    return high, low


def product(left, right):
    dot = functools.partial(jnp.dot, preferred_element_type=jnp.float32)
    return dot(left[0], right[0]) + (dot(left[0], right[1]) + dot(left[1], right[0]))


def own_kernel(at_ref, rows_ref, inverse_ref, high_ref, low_ref, panel_ref):
    inverse = split(inverse_ref[...])
    start = pl.multiple_of(at_ref[0] * 16, 16)
    for t in range(2):
        factor = product(inverse, split(rows_ref[:, t].reshape(256, 256)))
        high_ref[t], low_ref[t] = split(factor.T)
        panel_ref[t] = product(
            split(inverse_ref[pl.ds(start, 16), :]), split(rows_ref[:, t].reshape(256, 256))
        )


def column_kernel(mine_ref, inverse_ref, high_ref, low_ref):
    inverse = split(inverse_ref[...])
    for t in range(2):
        high_ref[t], low_ref[t] = split(product(inverse, split(mine_ref[:, t].reshape(256, 256))))


def update_kernel(at_ref, trailing_ref, high_ref, low_ref, mine_high, mine_low, other_ref, inverse_ref, out_ref, right_high, right_low, done, sems):
    def place(t, half, high, low):
        for part in range(2):
            start = pl.multiple_of((part * 4 + t * 2 + half) * 128, 128)
            right_high[:, pl.ds(start, 128)] = high[:, part * 128 : part * 128 + 128]
            right_low[:, pl.ds(start, 128)] = low[:, part * 128 : part * 128 + 128]

    inverse = split(inverse_ref[...])
    for t in range(2):
        place(t, at_ref[1], mine_high[t], mine_low[t])
        place(t, 1 - at_ref[1], *split(product(inverse, split(other_ref[:, t].reshape(256, 256)))))
    right = (right_high[...], right_low[...])
    copies = []
    for t in range(2):
        for i in range(256 // ROWS):
            rows = pl.ds(i * ROWS, ROWS)
            total = product((high_ref[t, rows], low_ref[t, rows]), right)
            for part in range(2):
                rows = pl.ds(i * ROWS + part * 64, 64)
                done[t, rows] = trailing_ref[t, rows] - total[part * 64 : part * 64 + 64].reshape(64, 8, 128)
                copy = pltpu.make_async_copy(done.at[t, rows], out_ref.at[t, rows], sems.at[len(copies)])
                copy.start()
                copies.append(copy)
    for copy in copies:
        copy.wait()


def on_device(trailing, panel, factor_inverse):
    col = lax.axis_index(COL)
    core = lax.axis_index("core")
    at = jnp.stack([col, core]).astype(jnp.int32)
    sliver = jnp.swapaxes(panel, 1, 2)
    sent = lax.ppermute(sliver, AXES, to_columns())
    quarter = gather_pairs(sliver[None], "yh")
    sent, quarter = lax.optimization_barrier((sent, quarter))
    many = jnp.broadcast_to(sent[None], (16, 2, 16, 256))
    mine = lax.all_to_all(many, ("z", "yl"), 0, 0, tiled=True)
    own = lax.all_gather(quarter, "x", axis=0, tiled=True)

    smem = pl.BlockSpec(memory_space=pltpu.SMEM)
    vmem = pl.BlockSpec(memory_space=pltpu.VMEM)
    high, low, factor_panel = pl.pallas_call(
        own_kernel,
        out_shape=[
            jax.ShapeDtypeStruct((2, 256, 256), jnp.bfloat16),
            jax.ShapeDtypeStruct((2, 256, 256), jnp.bfloat16),
            jax.ShapeDtypeStruct((2, 16, 256), jnp.float32),
        ],
        in_specs=[smem, vmem, vmem],
        out_specs=[vmem, vmem, vmem],
        compiler_params=pltpu.CompilerParams(vmem_limit_bytes=32 * 1024 * 1024),
    )(at, own, factor_inverse)

    mine, high, low = lax.optimization_barrier((mine, high, low))
    other = lax.ppermute(mine, "core", [(0, 1), (1, 0)])
    mine_high, mine_low = pl.pallas_call(
        column_kernel,
        out_shape=[jax.ShapeDtypeStruct((2, 256, 256), jnp.bfloat16)] * 2,
        in_specs=[vmem, vmem],
        out_specs=[vmem, vmem],
        compiler_params=pltpu.CompilerParams(vmem_limit_bytes=32 * 1024 * 1024),
    )(mine, factor_inverse)

    whole = trailing.reshape(2, 256, 4, 2, 128).swapaxes(2, 3).reshape(2, 256, 8, 128)
    updated = pl.pallas_call(
        update_kernel,
        out_shape=jax.ShapeDtypeStruct((2, 256, 8, 128), jnp.float32),
        in_specs=[smem] + [vmem] * 7,
        out_specs=pl.BlockSpec(memory_space=pl.ANY),
        scratch_shapes=[
            pltpu.VMEM((256, 1024), jnp.bfloat16),
            pltpu.VMEM((256, 1024), jnp.bfloat16),
            pltpu.VMEM((2, 256, 8, 128), jnp.float32),
            pltpu.SemaphoreType.DMA((512 // 64,)),
        ],
        compiler_params=pltpu.CompilerParams(vmem_limit_bytes=32 * 1024 * 1024),
    )(at, whole, high, low, mine_high, mine_low, other, factor_inverse)
    updated = updated.reshape(2, 256, 2, 4, 128).swapaxes(2, 3).reshape(2, 256, 4, 256)
    return updated, jnp.swapaxes(factor_panel, 1, 2)


def solution(mesh):
    fine = Mesh(mesh.devices.reshape(SIZES), AXES)
    specs = (P(None, ROW, None, COL), P(None, ROW, COL), P())
    return jax.shard_map(
        on_device, mesh=fine, in_specs=specs, out_specs=specs[:2], check_vma=False
    )
```
